32 devices in a mesh: slab: 4 (over y, core), tile: 8 (over z, x).
Axes of the slice: x: 2, y: 2, z: 4, core: 2. Of those that a mesh axis runs over, the one named last changes fastest.
Arguments:
- volume: float32 [768, 256, 128], P('tile', 'slab'), may hold values from 0 to 2
- footprints: bfloat16 [32, 128, 128], replicated, may hold values from -0.02734375 to 0.02734375
- foot_index: int32 [768, 8], P('tile'), may hold values from 0 to 31
- ray_block: int32 [768, 8], replicated, may hold values from 0 to 15, as said below
- ray_slot: int32 [16], replicated, may hold values from 0 to 15, as said below
- measured: float32 [16, 256, 128], P('tile', 'slab'), may hold values from -6 to 6
- weights: float32 [16, 256, 128], P('tile', 'slab'), may hold values from 0.25 to 4
Outputs:
- updated_volume: float32 [768, 256, 128], P('tile', 'slab')
The draws below stay inside these ranges and needn't reach their ends.
Inputs may be any that keep to these rules, and one draw needn't show every extreme that they name: A permutation of the 16 ray blocks; ray block b is held by index ray_slot[b] // 2 of tile, and its rows of measured and weights are row ray_slot[b]. `ray_block`: the crossings of the rows held by one index of tile name at most 4 distinct ray blocks, no two of them held by the same owner.
All inputs are finite; a program needn't handle non-finite values.
Results may differ from the reference program's by a relative error of at most 0.002.
Values may be sent and summed in bfloat16 or wider, within the bound.
A program may use at most 128 MiB of HBM per device.

```python
import math
import jax
import jax.numpy as jnp
from jax import lax

PX = 128
RAYS = 128
ROWS_DEV = 96
K = 8
NFOOT = 32
RB_DEV = 2
OWNERS = 8
RB = 16
TOUCH = 4
NROWS = 768
NZ = 256
N_TILE = 8


def crossing_tables(key):
    folded = jax.random.fold_in(key, 11)
    key_slot, key_owner, key_local, key_pick = jax.random.split(folded, 4)
    slot_table = jax.random.permutation(key_slot, RB).astype(jnp.int32)
    block_of_slot = jnp.argsort(slot_table).astype(jnp.int32)
    owner_keys = jax.random.split(key_owner, OWNERS)
    chosen = jax.vmap(lambda single: jax.random.permutation(single, OWNERS)[:TOUCH])(owner_keys)
    local_index = jax.random.randint(key_local, (OWNERS, TOUCH), 0, RB_DEV)
    touched = block_of_slot[chosen * RB_DEV + local_index]
    pick_keys = jax.random.split(key_pick, OWNERS)
    picks = jax.vmap(lambda single: jax.random.permutation(single, ROWS_DEV * K) % TOUCH)(pick_keys)
    blocks = jnp.take_along_axis(touched, picks, axis=1)
    return (slot_table, blocks.reshape(NROWS, K).astype(jnp.int32))


def draw_ray_slot(key, part):
    return crossing_tables(key)[0]


def draw_ray_block(key, part):
    return crossing_tables(key)[1]


def plant(array, rng, smallest, high):
    spot = [jax.random.randint(jax.random.fold_in(rng, axis), (), 0, length) for axis, length in enumerate(array.shape)]
    widest = array.shape.index(max(array.shape))
    beside = spot[:widest] + [(spot[widest] + 1) % array.shape[widest]] + spot[widest + 1:]
    return array.at[tuple(spot)].set(smallest).at[tuple(beside)].set(high)


def level_of(own_key, dims, cuts, smallest, high):
    def one(axis_at, parts):
        draws = jax.random.uniform(jax.random.fold_in(jax.random.fold_in(own_key, 6), axis_at), (parts,), jnp.float32, smallest / len(cuts), high / len(cuts))
        return jnp.repeat(jnp.exp(draws), dims[axis_at] // parts).reshape((-1,) + (1,) * (len(dims) - axis_at - 1))

    level = one(*cuts[0])
    for cut in cuts[1:]:
        level = level * one(*cut)
    return level


def scatter_about(stream_key, dims, scale, limit, cuts=(), dtype=jnp.bfloat16):
    array = scale * jax.random.normal(stream_key, dims, jnp.float32)
    if cuts:
        array = array * level_of(stream_key, dims, cuts, -0.22, 0.18)
    return jnp.clip(array, -limit, limit).astype(dtype)


def setup_inputs(seed: int = 0) -> dict:
    key_list = jax.random.split(jax.random.key(seed), 8)
    volume = jnp.clip(2.0 * jax.random.uniform(key_list[0], (NROWS, NZ, PX), jnp.float32) ** level_of(key_list[0], (NROWS, NZ, PX), ((0, 8), (1, 4)), -0.2, 0.2), 0.0, 2.0)
    footprints = scatter_about(key_list[1], (NFOOT, PX, RAYS), (PX * ROWS_DEV * K // RB_DEV) ** -0.5, 0.02734375)
    foot_index = plant(jax.random.randint(key_list[2], (NROWS, K), 0, NFOOT), jax.random.fold_in(key_list[2], 1), 0, NFOOT - 1).astype(jnp.int32)
    ray_block = draw_ray_block(jax.random.fold_in(key_list[7], 71), 0)
    ray_slot = draw_ray_slot(jax.random.fold_in(key_list[7], 71), 0)
    measured = scatter_about(key_list[5], (RB, NZ, RAYS), 1.0, 6.0, ((0, 8), (1, 4)), jnp.float32)
    weights = jnp.clip(jnp.exp(math.log(4.0) - 2.7725887 * jax.random.uniform(key_list[6], (RB, NZ, RAYS), jnp.float32) ** level_of(key_list[6], (RB, NZ, RAYS), ((0, 8), (1, 4)), -0.2, 0.2)), 0.25, 4.0)
    return dict(volume=volume, footprints=footprints, foot_index=foot_index, ray_block=ray_block, ray_slot=ray_slot, measured=measured, weights=weights)


smoothing = 0.04
step_length = 2.0
variation_weight = 1.0

def variation_gradient(density):
    grad_rows = jnp.concatenate([density[1:] - density[:-1], jnp.zeros_like(density[:1])], axis=0)
    grad_slices = jnp.concatenate([density[:, 1:] - density[:, :-1], jnp.zeros_like(density[:, :1])], axis=1)
    grad_cols = jnp.concatenate([density[:, :, 1:] - density[:, :, :-1], jnp.zeros_like(density[:, :, :1])], axis=2)
    magnitude = jnp.sqrt(grad_rows * grad_rows + grad_slices * grad_slices + grad_cols * grad_cols + smoothing)
    flux_rows = grad_rows / magnitude
    flux_slices = grad_slices / magnitude
    flux_cols = grad_cols / magnitude
    part_rows = jnp.concatenate([jnp.zeros_like(flux_rows[:1]), flux_rows[:-1]], axis=0) - flux_rows
    part_slices = jnp.concatenate([jnp.zeros_like(flux_slices[:, :1]), flux_slices[:, :-1]], axis=1) - flux_slices
    part_cols = jnp.concatenate([jnp.zeros_like(flux_cols[:, :, :1]), flux_cols[:, :, :-1]], axis=2) - flux_cols
    return part_rows + part_slices + part_cols

def reference(volume, footprints, foot_index, ray_block, ray_slot, measured, weights):
    row_total, slice_total, column_count = volume.shape
    ray_width = footprints.shape[2]
    crossings = ray_block.shape[1]
    slots = jnp.take(ray_slot, ray_block, axis=0).astype(jnp.int32)
    rounded = volume.astype(jnp.bfloat16)
    pixel_groups = rounded.reshape(N_TILE, ROWS_DEV, slice_total, column_count)
    offset_groups = foot_index.reshape(N_TILE, ROWS_DEV, crossings)
    slot_groups = slots.reshape(N_TILE, ROWS_DEV, crossings)

    def project(running_sum, inputs):
        pixels, offsets, targets = inputs
        stencil = jnp.take(footprints, offsets, axis=0).astype(jnp.float32)
        partial_value = jnp.einsum('rzp,rkpq->rkzq', pixels.astype(jnp.float32), stencil)
        running_sum = running_sum.at[targets.reshape(-1)].add(partial_value.reshape(-1, slice_total, ray_width))
        return (running_sum, None)
    start = jnp.zeros((ray_slot.shape[0], slice_total, ray_width), jnp.float32)
    projection, _ = lax.scan(project, start, (pixel_groups, offset_groups, slot_groups))
    residual = (weights * (projection - measured)).astype(jnp.bfloat16)

    def backproject(running, inputs):
        offsets, targets = inputs
        stencil = jnp.take(footprints, offsets, axis=0).astype(jnp.float32)
        values = jnp.take(residual, targets, axis=0).astype(jnp.float32)
        return (running, jnp.einsum('rkzq,rkpq->rzp', values, stencil))
    _, pieces = lax.scan(backproject, jnp.zeros((), jnp.float32), (offset_groups, slot_groups))
    data_grad = pieces.reshape(row_total, slice_total, column_count)
    updated = volume - step_length * (data_grad + variation_weight * variation_gradient(volume))
    return jnp.maximum(updated, 0.0)
```

```python
import functools
import math

import jax
import jax.numpy as jnp
from jax import lax
from jax.experimental import pallas as pl
from jax.experimental.pallas import tpu as pltpu
from jax.sharding import PartitionSpec as P

smoothing = 0.04
step_length = 2.0
variation_weight = 1.0

SUB = 8
WIDE = 256
WIRE = jnp.float32
VMEM_LIMIT = 56 * 2**20
MESH = pl.DeviceIdType.MESH
F32 = jnp.float32
BF16 = jnp.bfloat16


def iota(shape, axis):
    return lax.broadcasted_iota(jnp.int32, shape, axis)


def repeat_rows(x):
    rows, cols = x.shape
    tall = jnp.broadcast_to(x[:, None, :], (rows, SUB, cols)).reshape(rows * SUB, cols)
    keep = (iota(tall.shape, 0) & (SUB - 1)) == (iota(tall.shape, 1) & (SUB - 1))
    return jnp.where(keep, tall, 0.0).astype(BF16)


def dot(a, b):
    return lax.dot_general(a, b, (((1,), (0,)), ((), ())), preferred_element_type=F32)


def exchange_kernel(
    touch, owners, slabs, early,
    vol_ref, table_ref, index_ref, block_ref, slot_ref, meas_ref, wt_ref,
    base_out, back_out, resid_ref,
    vv, vb, fwd, bwd, base, edge_lo, edge_hi, next_z, prev_z, prev_flux,
    send, recv, back_send, back_recv,
    load_sem, out_sem, halo_send, halo_recv, part_send, part_recv, res_send, res_recv,
):
    rows, slices, px = vol_ref.shape
    rays = table_ref.shape[1]
    nfoot = table_ref.shape[0] // px
    crossings, all_rows = block_ref.shape
    owned = meas_ref.shape[0]
    keys = nfoot * touch
    zt = slices // SUB
    ts = touch * SUB
    pos = lax.axis_index("tile")
    layer = lax.axis_index("slab")
    t_next, t_prev = lax.rem(pos + 1, owners), lax.rem(pos + owners - 1, owners)
    z_next, z_prev = lax.rem(layer + 1, slabs), lax.rem(layer + slabs - 1, slabs)

    barrier = pltpu.get_barrier_semaphore()
    peers = [(layer, lax.rem(pos + d, owners)) for d in range(1, owners)]
    peers += [(z_next, pos), (z_prev, pos), (z_next, t_prev), (z_prev, t_next)]
    for peer in peers:
        pl.semaphore_signal(barrier, inc=1, device_id=peer, device_id_type=MESH)

    parts = 4
    piece = rows // parts
    loads = [
        pltpu.make_async_copy(
            vol_ref.at[pl.ds(c * piece, piece)], vv.at[pl.ds(1 + c * piece, piece)], load_sem.at[c]
        )
        for c in range(parts)
    ]
    for copy in loads:
        copy.start()

    blocks = block_ref[...]
    slot = jnp.zeros_like(blocks)
    for b in range(slot_ref.shape[0]):
        slot = jnp.where(blocks == b, slot_ref[b], slot)
    owner = slot >> (owned.bit_length() - 1) if owned & (owned - 1) == 0 else slot // owned
    local = jnp.where(owner == pos, slot - pos * owned, 0).astype(F32)
    locals_ = [
        jnp.max(local[:, n * rows : (n + 1) * rows], axis=(0, 1), keepdims=True)
        for n in range(owners)
    ]
    mine = (iota((all_rows, rows), 0) == iota((all_rows, rows), 1) + pos * rows).astype(BF16)
    my_owner = dot(owner.astype(BF16), mine)
    rank = jnp.zeros((1, 1), F32)
    compact = jnp.zeros_like(my_owner)
    place = []
    for o in range(owners):
        here = my_owner == o
        found = jnp.max(jnp.where(here, 1.0, 0.0), axis=(0, 1), keepdims=True)
        place.append([jnp.where(rank == t, found, 0.0) for t in range(touch)])
        compact = jnp.where(here, rank, compact)
        rank = rank + found
    key = index_ref[...] * touch + compact.astype(jnp.int32)
    ids = iota((keys, rows), 0)
    count = jnp.zeros((keys, rows), F32)
    for k in range(crossings):
        count = count + jnp.where(ids == key[k : k + 1, :], 1.0, 0.0)
    widen = (iota((rows, rows * SUB), 1) // SUB == iota((rows, rows * SUB), 0)).astype(BF16)
    spread = dot(count.astype(BF16), widen)
    step = WIDE // SUB
    for c in range(keys // step):
        fwd[c * WIDE : (c + 1) * WIDE, :] = repeat_rows(spread[c * step : (c + 1) * step])

    pl.semaphore_wait(barrier, len(peers))

    def remote(src, dst, sem_s, sem_r, peer):
        return pltpu.make_async_remote_copy(
            src_ref=src, dst_ref=dst, send_sem=sem_s, recv_sem=sem_r,
            device_id=peer, device_id_type=MESH,
        )

    def halo(i, src, dst, peer):
        return remote(src, dst, halo_send.at[i], halo_recv.at[i], peer)

    halos = [
        halo(0, vol_ref.at[pl.ds(0, 1)], vv.at[pl.ds(rows + 1, 1)], (layer, t_prev)),
        halo(1, vol_ref.at[pl.ds(rows - 1, 1)], vv.at[pl.ds(0, 1)], (layer, t_next)),
    ]
    for copy in halos:
        copy.start()

    for c in range(parts):
        loads[c].wait()
        for z in range(zt):
            part = vv[1 + c * piece : 1 + (c + 1) * piece, z * SUB : (z + 1) * SUB, :]
            vb[c * piece * SUB : (c + 1) * piece * SUB, z * px : (z + 1) * px] = part.reshape(
                piece * SUB, px
            ).astype(BF16)
    edge_lo[...] = vv[1 : rows + 1, 0, :]
    edge_hi[...] = vv[1 : rows + 1, slices - 1, :]
    more = [
        halo(2, edge_lo, next_z.at[pl.ds(0, rows)], (z_prev, pos)),
        halo(3, edge_hi, prev_z.at[pl.ds(0, rows)], (z_next, pos)),
        halo(4, edge_hi.at[pl.ds(0, SUB)], prev_z.at[pl.ds(rows, SUB)], (z_next, t_prev)),
        halo(5, edge_lo.at[pl.ds(rows - SUB, SUB)], next_z.at[pl.ds(rows, SUB)], (z_prev, t_next)),
    ]
    for copy in more:
        copy.start()
    halos += more

    per = WIDE // ts
    total = jnp.zeros((zt * ts, rays), F32)
    for c in range(nfoot // per):
        summed = dot(fwd[c * WIDE : (c + 1) * WIDE, :], vb[...])
        turned = jnp.concatenate(
            [
                jnp.concatenate(
                    [summed[f * ts : (f + 1) * ts, z * px : (z + 1) * px] for z in range(zt)], axis=0
                )
                for f in range(per)
            ],
            axis=1,
        ).astype(BF16)
        total = total + dot(turned, table_ref[c * per * px : (c + 1) * per * px, :])
    total = total.reshape(zt, touch, SUB, rays)
    partial = [total[:, t].reshape(slices, rays) for t in range(touch)]
    for o in range(owners):
        send[o] = sum(place[o][t] * partial[t] for t in range(touch)).astype(WIRE)

    there = []
    for d in range(1, owners):
        peer = lax.rem(pos + d, owners)
        there.append(
            remote(send.at[peer], recv.at[pos], part_send.at[d], part_recv.at[d], (layer, peer))
        )
    for copy in there:
        copy.start()
    recv[pl.ds(pos, 1)] = send[pl.ds(pos, 1)]

    for copy in halos:
        copy.wait_recv()
    last_row = pos == owners - 1
    last_slice = layer == slabs - 1
    sub = iota((slices, px), 0)
    lane = iota((slices, px), 1)

    def inverse(a, b, c):
        return lax.rsqrt(a * a + b * b + c * c + smoothing)

    def column(v, where):
        return jnp.where(where == px - 1, 0.0, pltpu.roll(v, px - 1, 1) - v)

    lower = prev_z[0:rows, :]
    g_z = edge_lo[...] - lower
    after = iota((rows, px), 0)
    below = pltpu.roll(lower, rows - 1, 0)
    below = jnp.where(after == rows - 1, prev_z[rows : rows + 1, :], below)
    g_r = jnp.where(jnp.logical_and(after == rows - 1, last_row), 0.0, below - lower)
    flux = g_z * inverse(g_r, g_z, column(lower, iota((rows, px), 1)))
    prev_flux[...] = jnp.where(layer == 0, 0.0, flux)

    def next_slice(v, edge):
        moved = jnp.where(sub == slices - 1, edge, pltpu.roll(v, slices - 1, 0)) - v
        return jnp.where(jnp.logical_and(sub == slices - 1, last_slice), 0.0, moved)

    before = vv[0]
    g_r = vv[1] - before
    g_z = next_slice(before, next_z[rows + SUB - 1 : rows + SUB, :])
    flux = g_r * inverse(g_r, g_z, column(before, lane))
    flux = jnp.where(pos == 0, 0.0, flux)

    def tv_row(r, flux):
        v = vv[r + 1]
        g_r = vv[r + 2] - v
        g_r = jnp.where(jnp.logical_and(r == rows - 1, last_row), 0.0, g_r)
        g_z = next_slice(v, next_z[pl.ds(r, 1), :])
        g_c = column(v, lane)
        inv = inverse(g_r, g_z, g_c)
        f_r, f_z, f_c = g_r * inv, g_z * inv, g_c * inv
        came = jnp.where(sub == 0, prev_flux[pl.ds(r, 1), :], pltpu.roll(f_z, 1, 0))
        variation = (flux - f_r) + (came - f_z) + (pltpu.roll(f_c, 1, 1) - f_c)
        base[r] = v - (step_length * variation_weight) * variation
        return f_r

    flux = lax.fori_loop(0, early, tv_row, flux)

    for copy in there:
        copy.wait_recv()
    residual = []
    for l in range(owned):
        own = sum(
            jnp.where(locals_[n] == l, 1.0, 0.0) * recv[n].astype(F32) for n in range(owners)
        )
        residual.append((wt_ref[l] * (own - meas_ref[l])).astype(BF16).astype(F32))
    for n in range(owners):
        picked = sum(jnp.where(locals_[n] == l, 1.0, 0.0) * residual[l] for l in range(owned))
        back_send[n] = picked.astype(BF16)
    home = []
    for d in range(1, owners):
        peer = lax.rem(pos + d, owners)
        home.append(
            remote(
                back_send.at[peer], back_recv.at[pos], res_send.at[d], res_recv.at[d], (layer, peer)
            )
        )
    for copy in home:
        copy.start()
    back_recv[pl.ds(pos, 1)] = back_send[pl.ds(pos, 1)]

    lax.fori_loop(early, rows, tv_row, flux)
    write_base = pltpu.make_async_copy(base, base_out, out_sem.at[0])
    write_base.start()

    widen = (iota((keys, keys * SUB), 1) // SUB == iota((keys, keys * SUB), 0)).astype(BF16)
    spread = dot(count.T.astype(BF16), widen)
    step = math.gcd(rows, 16)
    for c in range(rows // step):
        bwd[c * step * SUB : (c + 1) * step * SUB, :] = repeat_rows(
            spread[c * step : (c + 1) * step]
        )
    write_back = pltpu.make_async_copy(bwd, back_out, out_sem.at[1])
    write_back.start()

    for copy in home:
        copy.wait_recv()
    arrived = []
    for t in range(touch):
        one = sum(place[o][t] * back_recv[o].astype(F32) for o in range(owners))
        arrived.append(one.reshape(zt, SUB, rays))
    resid_ref[...] = jnp.stack(arrived, axis=1).reshape(zt * ts, rays).astype(BF16)
    write_base.wait()
    write_back.wait()
    for copy in halos + there + home:
        copy.wait_send()


def update_kernel(touch, resid_ref, table_ref, back_ref, base_ref, out_ref, grads):
    rows, slices, px = base_ref.shape
    nfoot = table_ref.shape[0] // px
    zt = slices // SUB
    ts = touch * SUB

    @pl.when(pl.program_id(0) == 0)
    def _():
        per = WIDE // px
        for c in range(nfoot // per):
            piece = lax.dot_general(
                resid_ref[...],
                table_ref[c * WIDE : (c + 1) * WIDE, :],
                (((1,), (1,)), ((), ())),
                preferred_element_type=F32,
            )
            for f in range(per):
                for z in range(zt):
                    at = (c * per + f) * ts
                    grads[at : at + ts, z * px : (z + 1) * px] = piece[
                        z * ts : (z + 1) * ts, f * px : (f + 1) * px
                    ].astype(BF16)

    grad = dot(back_ref[...], grads[...])
    for z in range(zt):
        at = slice(z * SUB, (z + 1) * SUB)
        one = grad[:, z * px : (z + 1) * px].reshape(rows, SUB, px)
        out_ref[:, at, :] = jnp.maximum(base_ref[:, at, :] - step_length * one, 0.0)


def per_device(owners, slabs, volume, footprints, foot_index, ray_block, ray_slot, measured, weights):
    rows, slices, px = volume.shape
    nfoot, _, rays = footprints.shape
    touch = owners // 2
    keys = nfoot * touch
    zt = slices // SUB
    table = footprints.reshape(nfoot * px, rays)
    any_space = pl.BlockSpec(memory_space=pl.ANY)
    vmem = pl.BlockSpec(memory_space=pltpu.VMEM)
    smem = pl.BlockSpec(memory_space=pltpu.SMEM)
    dma = pltpu.SemaphoreType.DMA
    base, back, resid = pl.pallas_call(
        functools.partial(exchange_kernel, touch, owners, slabs, rows // 2),
        out_shape=(
            jax.ShapeDtypeStruct(volume.shape, F32),
            jax.ShapeDtypeStruct((rows * SUB, keys * SUB), BF16),
            jax.ShapeDtypeStruct((zt * touch * SUB, rays), BF16),
        ),
        in_specs=[any_space, vmem, vmem, vmem, smem, vmem, vmem],
        out_specs=(any_space, any_space, vmem),
        scratch_shapes=[
            pltpu.VMEM((rows + 2, slices, px), F32),
            pltpu.VMEM((rows * SUB, zt * px), BF16),
            pltpu.VMEM((keys * SUB, rows * SUB), BF16),
            pltpu.VMEM((rows * SUB, keys * SUB), BF16),
            pltpu.VMEM((rows, slices, px), F32),
            pltpu.VMEM((rows, px), F32),
            pltpu.VMEM((rows, px), F32),
            pltpu.VMEM((rows + SUB, px), F32),
            pltpu.VMEM((rows + SUB, px), F32),
            pltpu.VMEM((rows, px), F32),
            pltpu.VMEM((owners, slices, rays), WIRE),
            pltpu.VMEM((owners, slices, rays), WIRE),
            pltpu.VMEM((owners, slices, rays), BF16),
            pltpu.VMEM((owners, slices, rays), BF16),
            dma((4,)),
            dma((2,)),
            dma((6,)),
            dma((6,)),
            dma((owners,)),
            dma((owners,)),
            dma((owners,)),
            dma((owners,)),
        ],
        compiler_params=pltpu.CompilerParams(
            collective_id=0, has_side_effects=True, vmem_limit_bytes=VMEM_LIMIT
        ),
    )(volume, table, foot_index.T, ray_block.T, ray_slot, measured, weights)
    steps = 4
    some = rows // steps
    return pl.pallas_call(
        functools.partial(update_kernel, touch),
        grid=(steps,),
        out_shape=jax.ShapeDtypeStruct(volume.shape, F32),
        in_specs=[
            pl.BlockSpec(resid.shape, lambda i: (0, 0)),
            pl.BlockSpec(table.shape, lambda i: (0, 0)),
            pl.BlockSpec((some * SUB, keys * SUB), lambda i: (i, 0)),
            pl.BlockSpec((some, slices, px), lambda i: (i, 0, 0)),
        ],
        out_specs=pl.BlockSpec((some, slices, px), lambda i: (i, 0, 0)),
        scratch_shapes=[pltpu.VMEM((keys * SUB, zt * px), BF16)],
        compiler_params=pltpu.CompilerParams(vmem_limit_bytes=VMEM_LIMIT),
    )(resid, table, back, base)


def solution(mesh):
    in_specs = (
        P("tile", "slab", None),
        P(),
        P("tile", None),
        P(),
        P(),
        P("tile", "slab", None),
        P("tile", "slab", None),
    )
    out_specs = P("tile", "slab", None)
    body = functools.partial(per_device, mesh.shape["tile"], mesh.shape["slab"])
    return jax.shard_map(body, mesh=mesh, in_specs=in_specs, out_specs=out_specs, check_vma=False)
```

```python
import functools
import math

import jax
import jax.numpy as jnp
from jax import lax
from jax.experimental import pallas as pl
from jax.experimental.pallas import tpu as pltpu
from jax.sharding import PartitionSpec as P

smoothing = 0.04
step_length = 2.0
variation_weight = 1.0

SUB = 8
WIDE = 256
WIRE = jnp.bfloat16
VMEM_LIMIT = 56 * 2**20
TOGETHER = 4
MESH = pl.DeviceIdType.MESH
F32 = jnp.float32
BF16 = jnp.bfloat16


def iota(shape, axis):
    return lax.broadcasted_iota(jnp.int32, shape, axis)


def repeat_rows(x):
    rows, cols = x.shape
    tall = jnp.broadcast_to(x[:, None, :], (rows, SUB, cols)).reshape(rows * SUB, cols)
    keep = (iota(tall.shape, 0) & (SUB - 1)) == (iota(tall.shape, 1) & (SUB - 1))
    return jnp.where(keep, tall, 0.0).astype(BF16)


def dot(a, b):
    return lax.dot_general(a, b, (((1,), (0,)), ((), ())), preferred_element_type=F32)


def exchange_kernel(
    touch, owners, slabs, early,
    vol_ref, table_hbm, index_ref, block_ref, slot_ref, meas_ref, wt_ref,
    base_out, back_out, resid_ref,
    table_ref, vv, vb, fwd, bwd, base, edge_lo, edge_hi, next_z, prev_z, prev_flux, upper,
    send, recv, back_send, back_recv,
    load_sem, out_sem, halo_send, halo_recv, part_send, part_recv, res_send, res_recv,
):
    rows, slices, px = vol_ref.shape
    rays = table_ref.shape[1]
    nfoot = table_ref.shape[0] // px
    crossings, all_rows = block_ref.shape
    owned = meas_ref.shape[0]
    keys = nfoot * touch
    zt = slices // SUB
    ts = touch * SUB
    pos = lax.axis_index("tile")
    layer = lax.axis_index("slab")
    t_next, t_prev = lax.rem(pos + 1, owners), lax.rem(pos + owners - 1, owners)
    z_next, z_prev = lax.rem(layer + 1, slabs), lax.rem(layer + slabs - 1, slabs)

    barrier = pltpu.get_barrier_semaphore()
    peers = [(layer, lax.rem(pos + d, owners)) for d in range(1, owners)]
    peers += [(z_next, pos), (z_prev, pos), (z_next, t_prev), (z_prev, t_next)]
    for peer in peers:
        pl.semaphore_signal(barrier, inc=1, device_id=peer, device_id_type=MESH)

    parts = 4
    piece = rows // parts
    loads = [
        pltpu.make_async_copy(
            vol_ref.at[pl.ds(c * piece, piece)], vv.at[pl.ds(1 + c * piece, piece)], load_sem.at[c]
        )
        for c in range(parts)
    ]
    for copy in loads:
        copy.start()
    load_table = pltpu.make_async_copy(table_hbm, table_ref, load_sem.at[parts])
    load_table.start()

    blocks = block_ref[...]
    slot = jnp.zeros_like(blocks)
    for b in range(slot_ref.shape[0]):
        slot = jnp.where(blocks == b, slot_ref[b], slot)
    owner = slot >> (owned.bit_length() - 1) if owned & (owned - 1) == 0 else slot // owned
    local = jnp.where(owner == pos, slot - pos * owned, 0).astype(F32)
    locals_ = [
        jnp.max(local[:, n * rows : (n + 1) * rows], axis=(0, 1), keepdims=True)
        for n in range(owners)
    ]
    mine = (iota((all_rows, rows), 0) == iota((all_rows, rows), 1) + pos * rows).astype(BF16)
    my_owner = dot(owner.astype(BF16), mine)
    rank = jnp.zeros((1, 1), F32)
    compact = jnp.zeros_like(my_owner)
    place = []
    for o in range(owners):
        here = my_owner == o
        found = jnp.max(jnp.where(here, 1.0, 0.0), axis=(0, 1), keepdims=True)
        place.append([jnp.where(rank == t, found, 0.0) for t in range(touch)])
        compact = jnp.where(here, rank, compact)
        rank = rank + found
    key = index_ref[...] * touch + compact.astype(jnp.int32)
    ids = iota((keys, rows), 0)
    count = jnp.zeros((keys, rows), F32)
    for k in range(crossings):
        count = count + jnp.where(ids == key[k : k + 1, :], 1.0, 0.0)
    widen = (iota((rows, rows * SUB), 1) // SUB == iota((rows, rows * SUB), 0)).astype(BF16)
    spread = dot(count.astype(BF16), widen)
    step = WIDE // SUB
    for c in range(keys // step):
        fwd[c * WIDE : (c + 1) * WIDE, :] = repeat_rows(spread[c * step : (c + 1) * step])

    pl.semaphore_wait(barrier, len(peers))

    def remote(src, dst, sem_s, sem_r, peer):
        return pltpu.make_async_remote_copy(
            src_ref=src, dst_ref=dst, send_sem=sem_s, recv_sem=sem_r,
            device_id=peer, device_id_type=MESH,
        )

    def halo(i, src, dst, peer):
        return remote(src, dst, halo_send.at[i], halo_recv.at[i], peer)

    halos = [
        halo(0, vol_ref.at[pl.ds(0, 1)], vv.at[pl.ds(rows + 1, 1)], (layer, t_prev)),
        halo(1, vol_ref.at[pl.ds(rows - 1, 1)], vv.at[pl.ds(0, 1)], (layer, t_next)),
    ]
    for copy in halos:
        copy.start()

    for c in range(parts):
        loads[c].wait()
        for z in range(zt):
            part = vv[1 + c * piece : 1 + (c + 1) * piece, z * SUB : (z + 1) * SUB, :]
            vb[c * piece * SUB : (c + 1) * piece * SUB, z * px : (z + 1) * px] = part.reshape(
                piece * SUB, px
            ).astype(BF16)
    edge_lo[...] = vv[1 : rows + 1, 0, :]
    edge_hi[...] = vv[1 : rows + 1, slices - 1, :]
    more = [
        halo(2, edge_lo, next_z.at[pl.ds(0, rows)], (z_prev, pos)),
        halo(3, edge_hi, prev_z.at[pl.ds(0, rows)], (z_next, pos)),
        halo(4, edge_hi.at[pl.ds(0, SUB)], prev_z.at[pl.ds(rows, SUB)], (z_next, t_prev)),
        halo(5, edge_lo.at[pl.ds(rows - SUB, SUB)], next_z.at[pl.ds(rows, SUB)], (z_prev, t_next)),
    ]
    for copy in more:
        copy.start()
    halos += more

    load_table.wait()

    per = WIDE // ts
    total = jnp.zeros((zt * ts, rays), F32)
    for c in range(nfoot // per):
        summed = dot(fwd[c * WIDE : (c + 1) * WIDE, :], vb[...])
        turned = jnp.concatenate(
            [
                jnp.concatenate(
                    [summed[f * ts : (f + 1) * ts, z * px : (z + 1) * px] for z in range(zt)], axis=0
                )
                for f in range(per)
            ],
            axis=1,
        ).astype(BF16)
        total = total + dot(turned, table_ref[c * per * px : (c + 1) * per * px, :])
    total = total.reshape(zt, touch, SUB, rays)
    partial = [total[:, t].reshape(slices, rays) for t in range(touch)]
    for o in range(owners):
        send[o] = sum(place[o][t] * partial[t] for t in range(touch)).astype(WIRE)

    there = []
    for d in range(1, owners):
        peer = lax.rem(pos + d, owners)
        there.append(
            remote(send.at[peer], recv.at[pos], part_send.at[d], part_recv.at[d], (layer, peer))
        )
    for copy in there:
        copy.start()
    recv[pl.ds(pos, 1)] = send[pl.ds(pos, 1)]

    last_row = pos == owners - 1
    last_slice = layer == slabs - 1
    sub = iota((slices, px), 0)
    lane = iota((slices, px), 1)
    after = iota((rows, px), 0)

    def inverse(a, b, c):
        return lax.rsqrt(a * a + b * b + c * c + smoothing)

    def column(v, where):
        return jnp.where(where == px - 1, 0.0, pltpu.roll(v, px - 1, 1) - v)

    def slice_flux(corner):
        lower = prev_z[0:rows, :]
        g_z = edge_lo[...] - lower
        below = pltpu.roll(lower, rows - 1, 0)
        if corner is not None:
            below = jnp.where(after == rows - 1, jnp.where(last_row, lower, corner), below)
        flux = g_z * inverse(below - lower, g_z, column(lower, iota((rows, px), 1)))
        prev_flux[...] = jnp.where(layer == 0, 0.0, flux)

    def next_slice(v, edge):
        return jnp.where(sub == slices - 1, edge, pltpu.roll(v, slices - 1, 0)) - v

    def tv_row(r, flux, v, below):
        g_r = below - v
        g_z = next_slice(v, upper[pl.ds(r, 1), :])
        g_c = column(v, lane)
        inv = inverse(g_r, g_z, g_c)
        f_r, f_z, f_c = g_r * inv, g_z * inv, g_c * inv
        came = jnp.where(sub == 0, prev_flux[pl.ds(r, 1), :], pltpu.roll(f_z, 1, 0))
        variation = (flux - f_r) + (came - f_z) + (pltpu.roll(f_c, 1, 1) - f_c)
        base[r] = v - (step_length * variation_weight) * variation
        return f_r

    def tv_rows(first, flux, final=False):
        for j in range(TOGETHER):
            v, below = vv[first + j + 1], vv[first + j + 2]
            if final and j == TOGETHER - 1:
                below = jnp.where(last_row, v, below)
            flux = tv_row(first + j, flux, v, below)
        return flux

    def tv_step(i, flux):
        return tv_rows(i * TOGETHER, flux)

    for copy in halos[2:4]:
        copy.wait_recv()
    upper[...] = jnp.where(last_slice, edge_hi[...], next_z[0:rows, :])
    slice_flux(None)
    flux = lax.fori_loop(0, early, tv_step, jnp.zeros((slices, px), F32))

    for copy in there:
        copy.wait_recv()
    residual = []
    for l in range(owned):
        own = sum(
            jnp.where(locals_[n] == l, 1.0, 0.0) * recv[n].astype(F32) for n in range(owners)
        )
        residual.append((wt_ref[l] * (own - meas_ref[l])).astype(BF16).astype(F32))
    for n in range(owners):
        picked = sum(jnp.where(locals_[n] == l, 1.0, 0.0) * residual[l] for l in range(owned))
        back_send[n] = picked.astype(BF16)
    home = []
    for d in range(1, owners):
        peer = lax.rem(pos + d, owners)
        home.append(
            remote(
                back_send.at[peer], back_recv.at[pos], res_send.at[d], res_recv.at[d], (layer, peer)
            )
        )
    for copy in home:
        copy.start()
    back_recv[pl.ds(pos, 1)] = back_send[pl.ds(pos, 1)]

    for copy in halos[:2] + halos[4:]:
        copy.wait_recv()
    slice_flux(prev_z[rows : rows + 1, :])
    before = vv[0]
    corner = jnp.where(last_slice, before[slices - 1 : slices, :], next_z[rows + SUB - 1 : rows + SUB, :])
    g_r = vv[1] - before
    came = g_r * inverse(g_r, next_slice(before, corner), column(before, lane))
    base[0] = base[0] - (step_length * variation_weight) * jnp.where(pos == 0, 0.0, came)
    steps = rows // TOGETHER
    flux = lax.fori_loop(early, steps - 1, tv_step, flux)
    tv_rows((steps - 1) * TOGETHER, flux, True)
    write_base = pltpu.make_async_copy(base, base_out, out_sem.at[0])
    write_base.start()

    widen = (iota((keys, keys * SUB), 1) // SUB == iota((keys, keys * SUB), 0)).astype(BF16)
    spread = dot(count.T.astype(BF16), widen)
    step = math.gcd(rows, 16)
    for c in range(rows // step):
        bwd[c * step * SUB : (c + 1) * step * SUB, :] = repeat_rows(
            spread[c * step : (c + 1) * step]
        )
    write_back = pltpu.make_async_copy(bwd, back_out, out_sem.at[1])
    write_back.start()

    for copy in home:
        copy.wait_recv()
    arrived = []
    for t in range(touch):
        one = sum(place[o][t] * back_recv[o].astype(F32) for o in range(owners))
        arrived.append(one.reshape(zt, SUB, rays))
    resid_ref[...] = jnp.stack(arrived, axis=1).reshape(zt * ts, rays).astype(BF16)
    write_base.wait()
    write_back.wait()
    for copy in halos + there + home:
        copy.wait_send()


def update_kernel(touch, resid_ref, table_ref, back_ref, base_ref, out_ref, grads):
    rows, slices, px = base_ref.shape
    nfoot = table_ref.shape[0] // px
    zt = slices // SUB
    ts = touch * SUB

    @pl.when(pl.program_id(0) == 0)
    def _():
        per = WIDE // px
        for c in range(nfoot // per):
            piece = lax.dot_general(
                resid_ref[...],
                table_ref[c * WIDE : (c + 1) * WIDE, :],
                (((1,), (1,)), ((), ())),
                preferred_element_type=F32,
            )
            for f in range(per):
                for z in range(zt):
                    at = (c * per + f) * ts
                    grads[at : at + ts, z * px : (z + 1) * px] = piece[
                        z * ts : (z + 1) * ts, f * px : (f + 1) * px
                    ].astype(BF16)

    grad = dot(back_ref[...], grads[...])
    for z in range(zt):
        at = slice(z * SUB, (z + 1) * SUB)
        one = grad[:, z * px : (z + 1) * px].reshape(rows, SUB, px)
        out_ref[:, at, :] = jnp.maximum(base_ref[:, at, :] - step_length * one, 0.0)


def per_device(owners, slabs, volume, footprints, foot_index, ray_block, ray_slot, measured, weights):
    rows, slices, px = volume.shape
    nfoot, _, rays = footprints.shape
    touch = owners // 2
    keys = nfoot * touch
    zt = slices // SUB
    table = footprints.reshape(nfoot * px, rays)
    any_space = pl.BlockSpec(memory_space=pl.ANY)
    vmem = pl.BlockSpec(memory_space=pltpu.VMEM)
    smem = pl.BlockSpec(memory_space=pltpu.SMEM)
    dma = pltpu.SemaphoreType.DMA
    base, back, resid = pl.pallas_call(
        functools.partial(exchange_kernel, touch, owners, slabs, rows // TOGETHER // 2),
        out_shape=(
            jax.ShapeDtypeStruct(volume.shape, F32),
            jax.ShapeDtypeStruct((rows * SUB, keys * SUB), BF16),
            jax.ShapeDtypeStruct((zt * touch * SUB, rays), BF16),
        ),
        in_specs=[any_space, any_space, vmem, vmem, smem, vmem, vmem],
        out_specs=(any_space, any_space, vmem),
        scratch_shapes=[
            pltpu.VMEM(table.shape, BF16),
            pltpu.VMEM((rows + 2, slices, px), F32),
            pltpu.VMEM((rows * SUB, zt * px), BF16),
            pltpu.VMEM((keys * SUB, rows * SUB), BF16),
            pltpu.VMEM((rows * SUB, keys * SUB), BF16),
            pltpu.VMEM((rows, slices, px), F32),
            pltpu.VMEM((rows, px), F32),
            pltpu.VMEM((rows, px), F32),
            pltpu.VMEM((rows + SUB, px), F32),
            pltpu.VMEM((rows + SUB, px), F32),
            pltpu.VMEM((rows, px), F32),
            pltpu.VMEM((rows, px), F32),
            pltpu.VMEM((owners, slices, rays), WIRE),
            pltpu.VMEM((owners, slices, rays), WIRE),
            pltpu.VMEM((owners, slices, rays), BF16),
            pltpu.VMEM((owners, slices, rays), BF16),
            dma((5,)),
            dma((2,)),
            dma((6,)),
            dma((6,)),
            dma((owners,)),
            dma((owners,)),
            dma((owners,)),
            dma((owners,)),
        ],
        compiler_params=pltpu.CompilerParams(
            collective_id=0, has_side_effects=True, vmem_limit_bytes=VMEM_LIMIT
        ),
    )(volume, table, foot_index.T, ray_block.T, ray_slot, measured, weights)
    steps = 4
    some = rows // steps
    return pl.pallas_call(
        functools.partial(update_kernel, touch),
        grid=(steps,),
        out_shape=jax.ShapeDtypeStruct(volume.shape, F32),
        in_specs=[
            pl.BlockSpec(resid.shape, lambda i: (0, 0)),
            pl.BlockSpec(table.shape, lambda i: (0, 0)),
            pl.BlockSpec((some * SUB, keys * SUB), lambda i: (i, 0)),
            pl.BlockSpec((some, slices, px), lambda i: (i, 0, 0)),
        ],
        out_specs=pl.BlockSpec((some, slices, px), lambda i: (i, 0, 0)),
        scratch_shapes=[pltpu.VMEM((keys * SUB, zt * px), BF16)],
        compiler_params=pltpu.CompilerParams(vmem_limit_bytes=VMEM_LIMIT),
    )(resid, table, back, base)


def solution(mesh):
    in_specs = (
        P("tile", "slab", None),
        P(),
        P("tile", None),
        P(),
        P(),
        P("tile", "slab", None),
        P("tile", "slab", None),
    )
    out_specs = P("tile", "slab", None)
    body = functools.partial(per_device, mesh.shape["tile"], mesh.shape["slab"])
    return jax.shard_map(body, mesh=mesh, in_specs=in_specs, out_specs=out_specs, check_vma=False)
```

```python
import functools
import math

import jax
import jax.numpy as jnp
from jax import lax
from jax.experimental import pallas as pl
from jax.experimental.pallas import tpu as pltpu
from jax.sharding import PartitionSpec as P

smoothing = 0.04
step_length = 2.0
variation_weight = 1.0

SUB = 8
WIDE = 256
WIRE = jnp.bfloat16
VMEM_LIMIT = 56 * 2**20
TOGETHER = 4
MESH = pl.DeviceIdType.MESH
F32 = jnp.float32
BF16 = jnp.bfloat16


def iota(shape, axis):
    return lax.broadcasted_iota(jnp.int32, shape, axis)


def repeat_rows(x):
    rows, cols = x.shape
    tall = jnp.broadcast_to(x[:, None, :], (rows, SUB, cols)).reshape(rows * SUB, cols)
    keep = (iota(tall.shape, 0) & (SUB - 1)) == (iota(tall.shape, 1) & (SUB - 1))
    return jnp.where(keep, tall, 0.0).astype(BF16)


def dot(a, b):
    return lax.dot_general(a, b, (((1,), (0,)), ((), ())), preferred_element_type=F32)


def exchange_kernel(
    touch, owners, slabs, early,
    vol_ref, table_hbm, index_ref, block_ref, slot_ref, meas_ref, wt_ref,
    base_out, back_out, resid_ref,
    table_ref, vv, vb, turned, fwd, bwd, base, edge_lo, edge_hi, next_z, prev_z, prev_flux, upper,
    send, recv, back_send, back_recv,
    load_sem, out_sem, halo_send, halo_recv, part_send, part_recv, res_send, res_recv,
):
    rows, slices, px = vol_ref.shape
    rays = table_ref.shape[1]
    nfoot = table_ref.shape[0] // px
    crossings, all_rows = block_ref.shape
    owned = meas_ref.shape[0]
    keys = nfoot * touch
    zt = slices // SUB
    ts = touch * SUB
    pos = lax.axis_index("tile")
    layer = lax.axis_index("slab")
    t_next, t_prev = lax.rem(pos + 1, owners), lax.rem(pos + owners - 1, owners)
    z_next, z_prev = lax.rem(layer + 1, slabs), lax.rem(layer + slabs - 1, slabs)

    barrier = pltpu.get_barrier_semaphore()
    peers = [(layer, lax.rem(pos + d, owners)) for d in range(1, owners)]
    peers += [(z_next, pos), (z_prev, pos), (z_next, t_prev), (z_prev, t_next)]
    for peer in peers:
        pl.semaphore_signal(barrier, inc=1, device_id=peer, device_id_type=MESH)

    tiles = WIDE // px
    parts = zt // tiles
    some = tiles * SUB
    loads = [
        pltpu.make_async_copy(
            vol_ref.at[:, pl.ds(c * some, some)],
            vv.at[pl.ds(1, rows), pl.ds(c * some, some)],
            load_sem.at[c],
        )
        for c in range(parts)
    ]
    for copy in loads:
        copy.start()
    load_table = pltpu.make_async_copy(table_hbm, table_ref, load_sem.at[parts])
    load_table.start()

    blocks = block_ref[...]
    slot = jnp.zeros_like(blocks)
    for b in range(slot_ref.shape[0]):
        slot = jnp.where(blocks == b, slot_ref[b], slot)
    owner = slot >> (owned.bit_length() - 1) if owned & (owned - 1) == 0 else slot // owned
    local = jnp.where(owner == pos, slot - pos * owned, 0).astype(F32)
    locals_ = [
        jnp.max(local[:, n * rows : (n + 1) * rows], axis=(0, 1), keepdims=True)
        for n in range(owners)
    ]
    mine = (iota((all_rows, rows), 0) == iota((all_rows, rows), 1) + pos * rows).astype(BF16)
    my_owner = dot(owner.astype(BF16), mine)
    rank = jnp.zeros((1, 1), F32)
    compact = jnp.zeros_like(my_owner)
    place = []
    for o in range(owners):
        here = my_owner == o
        found = jnp.max(jnp.where(here, 1.0, 0.0), axis=(0, 1), keepdims=True)
        place.append([jnp.where(rank == t, found, 0.0) for t in range(touch)])
        compact = jnp.where(here, rank, compact)
        rank = rank + found
    key = index_ref[...] * touch + compact.astype(jnp.int32)
    ids = iota((keys, rows), 0)
    count = jnp.zeros((keys, rows), F32)
    for k in range(crossings):
        count = count + jnp.where(ids == key[k : k + 1, :], 1.0, 0.0)
    widen = (iota((rows, rows * SUB), 1) // SUB == iota((rows, rows * SUB), 0)).astype(BF16)
    spread = dot(count.astype(BF16), widen)
    step = WIDE // SUB
    for c in range(keys // step):
        fwd[c * WIDE : (c + 1) * WIDE, :] = repeat_rows(spread[c * step : (c + 1) * step])

    pl.semaphore_wait(barrier, len(peers))

    def remote(src, dst, sem_s, sem_r, peer):
        return pltpu.make_async_remote_copy(
            src_ref=src, dst_ref=dst, send_sem=sem_s, recv_sem=sem_r,
            device_id=peer, device_id_type=MESH,
        )

    def halo(i, src, dst, peer):
        return remote(src, dst, halo_send.at[i], halo_recv.at[i], peer)

    halos = [
        halo(0, vol_ref.at[pl.ds(0, 1)], vv.at[pl.ds(rows + 1, 1)], (layer, t_prev)),
        halo(1, vol_ref.at[pl.ds(rows - 1, 1)], vv.at[pl.ds(0, 1)], (layer, t_next)),
    ]
    for copy in halos:
        copy.start()

    for c in range(parts):
        loads[c].wait()
        for z in range(c * tiles, (c + 1) * tiles):
            part = vv[1 : rows + 1, z * SUB : (z + 1) * SUB, :]
            vb[:, z * px : (z + 1) * px] = part.reshape(rows * SUB, px).astype(BF16)
        more = []
        if c == 0:
            edge_lo[...] = vv[1 : rows + 1, 0, :]
            more += [
                halo(2, edge_lo, next_z.at[pl.ds(0, rows)], (z_prev, pos)),
                halo(4, edge_lo.at[pl.ds(rows - SUB, SUB)], next_z.at[pl.ds(rows, SUB)], (z_prev, t_next)),
            ]
        if c == parts - 1:
            edge_hi[...] = vv[1 : rows + 1, slices - 1, :]
            more += [
                halo(3, edge_hi, prev_z.at[pl.ds(0, rows)], (z_next, pos)),
                halo(5, edge_hi.at[pl.ds(0, SUB)], prev_z.at[pl.ds(rows, SUB)], (z_next, t_prev)),
            ]
        for copy in more:
            copy.start()
        halos += more
        summed = dot(fwd[...], vb[:, c * WIDE : (c + 1) * WIDE]).astype(BF16)
        for f in range(nfoot):
            for j in range(tiles):
                at = (c * tiles + j) * ts
                turned[at : at + ts, f * px : (f + 1) * px] = summed[
                    f * ts : (f + 1) * ts, j * px : (j + 1) * px
                ]
    slab_halos = [halos[2], halos[4]]
    tile_halos = [halos[0], halos[1], halos[3], halos[5]]
    load_table.wait()
    total = dot(turned[...], table_ref[...])
    total = total.reshape(zt, touch, SUB, rays)
    partial = [total[:, t].reshape(slices, rays) for t in range(touch)]
    for o in range(owners):
        send[o] = sum(place[o][t] * partial[t] for t in range(touch)).astype(WIRE)

    there = []
    for d in range(1, owners):
        peer = lax.rem(pos + d, owners)
        there.append(
            remote(send.at[peer], recv.at[pos], part_send.at[d], part_recv.at[d], (layer, peer))
        )
    for copy in there:
        copy.start()
    recv[pl.ds(pos, 1)] = send[pl.ds(pos, 1)]

    last_row = pos == owners - 1
    last_slice = layer == slabs - 1
    sub = iota((slices, px), 0)
    lane = iota((slices, px), 1)
    after = iota((rows, px), 0)

    def inverse(a, b, c):
        return lax.rsqrt(a * a + b * b + c * c + smoothing)

    def column(v, where):
        return jnp.where(where == px - 1, 0.0, pltpu.roll(v, px - 1, 1) - v)

    def slice_flux(corner):
        lower = prev_z[0:rows, :]
        g_z = edge_lo[...] - lower
        below = pltpu.roll(lower, rows - 1, 0)
        if corner is not None:
            below = jnp.where(after == rows - 1, jnp.where(last_row, lower, corner), below)
        flux = g_z * inverse(below - lower, g_z, column(lower, iota((rows, px), 1)))
        prev_flux[...] = jnp.where(layer == 0, 0.0, flux)

    def next_slice(v, edge):
        return jnp.where(sub == slices - 1, edge, pltpu.roll(v, slices - 1, 0)) - v

    def tv_row(r, flux, v, below):
        g_r = below - v
        g_z = next_slice(v, upper[pl.ds(r, 1), :])
        g_c = column(v, lane)
        inv = inverse(g_r, g_z, g_c)
        f_r, f_z, f_c = g_r * inv, g_z * inv, g_c * inv
        came = jnp.where(sub == 0, prev_flux[pl.ds(r, 1), :], pltpu.roll(f_z, 1, 0))
        variation = (flux - f_r) + (came - f_z) + (pltpu.roll(f_c, 1, 1) - f_c)
        base[r] = v - (step_length * variation_weight) * variation
        return f_r

    def tv_rows(first, flux, final=False):
        for j in range(TOGETHER):
            v, below = vv[first + j + 1], vv[first + j + 2]
            if final and j == TOGETHER - 1:
                below = jnp.where(last_row, v, below)
            flux = tv_row(first + j, flux, v, below)
        return flux

    def tv_step(i, flux):
        return tv_rows(i * TOGETHER, flux)

    for copy in slab_halos:
        copy.wait_recv()
    upper[...] = jnp.where(last_slice, edge_hi[...], next_z[0:rows, :])
    slice_flux(None)
    flux = lax.fori_loop(0, early, tv_step, jnp.zeros((slices, px), F32))

    for copy in there:
        copy.wait_recv()
    residual = []
    for l in range(owned):
        own = sum(
            jnp.where(locals_[n] == l, 1.0, 0.0) * recv[n].astype(F32) for n in range(owners)
        )
        residual.append((wt_ref[l] * (own - meas_ref[l])).astype(BF16).astype(F32))
    for n in range(owners):
        picked = sum(jnp.where(locals_[n] == l, 1.0, 0.0) * residual[l] for l in range(owned))
        back_send[n] = picked.astype(BF16)
    home = []
    for d in range(1, owners):
        peer = lax.rem(pos + d, owners)
        home.append(
            remote(
                back_send.at[peer], back_recv.at[pos], res_send.at[d], res_recv.at[d], (layer, peer)
            )
        )
    for copy in home:
        copy.start()
    back_recv[pl.ds(pos, 1)] = back_send[pl.ds(pos, 1)]

    for copy in tile_halos:
        copy.wait_recv()
    slice_flux(prev_z[rows : rows + 1, :])
    before = vv[0]
    corner = jnp.where(last_slice, before[slices - 1 : slices, :], next_z[rows + SUB - 1 : rows + SUB, :])
    g_r = vv[1] - before
    came = g_r * inverse(g_r, next_slice(before, corner), column(before, lane))
    base[0] = base[0] - (step_length * variation_weight) * jnp.where(pos == 0, 0.0, came)
    steps = rows // TOGETHER
    flux = lax.fori_loop(early, steps - 1, tv_step, flux)
    tv_rows((steps - 1) * TOGETHER, flux, True)
    write_base = pltpu.make_async_copy(base, base_out, out_sem.at[0])
    write_base.start()

    widen = (iota((keys, keys * SUB), 1) // SUB == iota((keys, keys * SUB), 0)).astype(BF16)
    spread = dot(count.T.astype(BF16), widen)
    step = math.gcd(rows, 16)
    for c in range(rows // step):
        bwd[c * step * SUB : (c + 1) * step * SUB, :] = repeat_rows(
            spread[c * step : (c + 1) * step]
        )
    write_back = pltpu.make_async_copy(bwd, back_out, out_sem.at[1])
    write_back.start()

    for copy in home:
        copy.wait_recv()
    arrived = []
    for t in range(touch):
        one = sum(place[o][t] * back_recv[o].astype(F32) for o in range(owners))
        arrived.append(one.reshape(zt, SUB, rays))
    resid_ref[...] = jnp.stack(arrived, axis=1).reshape(zt * ts, rays).astype(BF16)
    write_base.wait()
    write_back.wait()
    for copy in halos + there + home:
        copy.wait_send()


def update_kernel(touch, resid_ref, table_ref, back_hbm, base_ref, out_ref, back_ref, grads, sem):
    rows, some, px = base_ref.shape
    nfoot = table_ref.shape[0] // px
    steps = grads.shape[0]
    tiles = some // SUB
    ts = touch * SUB
    load = pltpu.make_async_copy(back_hbm, back_ref, sem)

    @pl.when(pl.program_id(0) == 0)
    def _():
        load.start()
        per = WIDE // px
        for c in range(nfoot // per):
            piece = lax.dot_general(
                resid_ref[...],
                table_ref[c * WIDE : (c + 1) * WIDE, :],
                (((1,), (1,)), ((), ())),
                preferred_element_type=F32,
            ).astype(BF16)
            for f in range(per):
                at = (c * per + f) * ts
                for z in range(steps * tiles):
                    j = z % tiles
                    grads[z // tiles, at : at + ts, j * px : (j + 1) * px] = piece[
                        z * ts : (z + 1) * ts, f * px : (f + 1) * px
                    ]
        load.wait()

    grad = dot(back_ref[...], grads[pl.program_id(0)])
    for z in range(tiles):
        at = slice(z * SUB, (z + 1) * SUB)
        one = grad[:, z * px : (z + 1) * px].reshape(rows, SUB, px)
        out_ref[:, at, :] = jnp.maximum(base_ref[:, at, :] - step_length * one, 0.0)


def per_device(owners, slabs, volume, footprints, foot_index, ray_block, ray_slot, measured, weights):
    rows, slices, px = volume.shape
    nfoot, _, rays = footprints.shape
    touch = owners // 2
    keys = nfoot * touch
    zt = slices // SUB
    table = footprints.reshape(nfoot * px, rays)
    any_space = pl.BlockSpec(memory_space=pl.ANY)
    vmem = pl.BlockSpec(memory_space=pltpu.VMEM)
    smem = pl.BlockSpec(memory_space=pltpu.SMEM)
    dma = pltpu.SemaphoreType.DMA
    base, back, resid = pl.pallas_call(
        functools.partial(exchange_kernel, touch, owners, slabs, rows // TOGETHER // 2),
        out_shape=(
            jax.ShapeDtypeStruct(volume.shape, F32),
            jax.ShapeDtypeStruct((rows * SUB, keys * SUB), BF16),
            jax.ShapeDtypeStruct((zt * touch * SUB, rays), BF16),
        ),
        in_specs=[any_space, any_space, vmem, vmem, smem, vmem, vmem],
        out_specs=(any_space, any_space, vmem),
        scratch_shapes=[
            pltpu.VMEM(table.shape, BF16),
            pltpu.VMEM((rows + 2, slices, px), F32),
            pltpu.VMEM((rows * SUB, zt * px), BF16),
            pltpu.VMEM((zt * touch * SUB, nfoot * px), BF16),
            pltpu.VMEM((keys * SUB, rows * SUB), BF16),
            pltpu.VMEM((rows * SUB, keys * SUB), BF16),
            pltpu.VMEM((rows, slices, px), F32),
            pltpu.VMEM((rows, px), F32),
            pltpu.VMEM((rows, px), F32),
            pltpu.VMEM((rows + SUB, px), F32),
            pltpu.VMEM((rows + SUB, px), F32),
            pltpu.VMEM((rows, px), F32),
            pltpu.VMEM((rows, px), F32),
            pltpu.VMEM((owners, slices, rays), WIRE),
            pltpu.VMEM((owners, slices, rays), WIRE),
            pltpu.VMEM((owners, slices, rays), BF16),
            pltpu.VMEM((owners, slices, rays), BF16),
            dma((zt * px // WIDE + 1,)),
            dma((2,)),
            dma((6,)),
            dma((6,)),
            dma((owners,)),
            dma((owners,)),
            dma((owners,)),
            dma((owners,)),
        ],
        compiler_params=pltpu.CompilerParams(
            collective_id=0, has_side_effects=True, vmem_limit_bytes=VMEM_LIMIT
        ),
    )(volume, table, foot_index.T, ray_block.T, ray_slot, measured, weights)
    some = WIDE // px * SUB
    steps = slices // some
    return pl.pallas_call(
        functools.partial(update_kernel, touch),
        grid=(steps,),
        out_shape=jax.ShapeDtypeStruct(volume.shape, F32),
        in_specs=[
            pl.BlockSpec(resid.shape, lambda i: (0, 0)),
            pl.BlockSpec(table.shape, lambda i: (0, 0)),
            any_space,
            pl.BlockSpec((rows, some, px), lambda i: (0, i, 0)),
        ],
        out_specs=pl.BlockSpec((rows, some, px), lambda i: (0, i, 0)),
        scratch_shapes=[
            pltpu.VMEM(back.shape, BF16),
            pltpu.VMEM((steps, keys * SUB, WIDE), BF16),
            dma(()),
        ],
        compiler_params=pltpu.CompilerParams(vmem_limit_bytes=VMEM_LIMIT),
    )(resid, table, back, base)


def solution(mesh):
    in_specs = (
        P("tile", "slab", None),
        P(),
        P("tile", None),
        P(),
        P(),
        P("tile", "slab", None),
        P("tile", "slab", None),
    )
    out_specs = P("tile", "slab", None)
    body = functools.partial(per_device, mesh.shape["tile"], mesh.shape["slab"])
    return jax.shard_map(body, mesh=mesh, in_specs=in_specs, out_specs=out_specs, check_vma=False)
```

```python
import functools
import math

import jax
import jax.numpy as jnp
from jax import lax
from jax.experimental import pallas as pl
from jax.experimental.pallas import tpu as pltpu
from jax.sharding import PartitionSpec as P

smoothing = 0.04
step_length = 2.0
variation_weight = 1.0

SUB = 8
WIDE = 256
WIRE = jnp.bfloat16
VMEM_LIMIT = 56 * 2**20
TOGETHER = 4
MESH = pl.DeviceIdType.MESH
F32 = jnp.float32
BF16 = jnp.bfloat16


def iota(shape, axis):
    return lax.broadcasted_iota(jnp.int32, shape, axis)


def repeat_rows(x):
    rows, cols = x.shape
    tall = jnp.broadcast_to(x[:, None, :], (rows, SUB, cols)).reshape(rows * SUB, cols)
    keep = (iota(tall.shape, 0) & (SUB - 1)) == (iota(tall.shape, 1) & (SUB - 1))
    return jnp.where(keep, tall, 0.0).astype(BF16)


def dot(a, b):
    return lax.dot_general(a, b, (((1,), (0,)), ((), ())), preferred_element_type=F32)


def exchange_kernel(
    touch, owners, slabs, early,
    vol_ref, table_hbm, index_ref, block_ref, slot_ref, meas_ref, wt_ref,
    base_out, back_out, resid_ref,
    table_ref, vv, vb, fwd, bwd, base, edge_lo, edge_hi, next_z, prev_z, prev_flux, upper,
    send, recv, back_send, back_recv,
    load_sem, out_sem, halo_send, halo_recv, part_send, part_recv, res_send, res_recv,
):
    rows, slices, px = vol_ref.shape
    rays = table_ref.shape[1]
    nfoot = table_ref.shape[0] // px
    crossings, all_rows = block_ref.shape
    owned = meas_ref.shape[0]
    keys = nfoot * touch
    zt = slices // SUB
    ts = touch * SUB
    pos = lax.axis_index("tile")
    layer = lax.axis_index("slab")
    t_next, t_prev = lax.rem(pos + 1, owners), lax.rem(pos + owners - 1, owners)
    z_next, z_prev = lax.rem(layer + 1, slabs), lax.rem(layer + slabs - 1, slabs)

    barrier = pltpu.get_barrier_semaphore()
    peers = [(layer, lax.rem(pos + d, owners)) for d in range(1, owners)]
    peers += [(z_next, pos), (z_prev, pos), (z_next, t_prev), (z_prev, t_next)]
    for peer in peers:
        pl.semaphore_signal(barrier, inc=1, device_id=peer, device_id_type=MESH)

    parts = 4
    piece = rows // parts
    loads = [
        pltpu.make_async_copy(
            vol_ref.at[pl.ds(c * piece, piece)], vv.at[pl.ds(1 + c * piece, piece)], load_sem.at[c]
        )
        for c in range(parts)
    ]
    for copy in loads:
        copy.start()
    load_table = pltpu.make_async_copy(table_hbm, table_ref, load_sem.at[parts])
    load_table.start()

    blocks = block_ref[...]
    slot = jnp.zeros_like(blocks)
    for b in range(slot_ref.shape[0]):
        slot = jnp.where(blocks == b, slot_ref[b], slot)
    owner = slot >> (owned.bit_length() - 1) if owned & (owned - 1) == 0 else slot // owned
    local = jnp.where(owner == pos, slot - pos * owned, 0).astype(F32)
    locals_ = [
        jnp.max(local[:, n * rows : (n + 1) * rows], axis=(0, 1), keepdims=True)
        for n in range(owners)
    ]
    mine = (iota((all_rows, rows), 0) == iota((all_rows, rows), 1) + pos * rows).astype(BF16)
    my_owner = dot(owner.astype(BF16), mine)
    rank = jnp.zeros((1, 1), F32)
    compact = jnp.zeros_like(my_owner)
    place = []
    for o in range(owners):
        here = my_owner == o
        found = jnp.max(jnp.where(here, 1.0, 0.0), axis=(0, 1), keepdims=True)
        place.append([jnp.where(rank == t, found, 0.0) for t in range(touch)])
        compact = jnp.where(here, rank, compact)
        rank = rank + found
    key = index_ref[...] * touch + compact.astype(jnp.int32)
    ids = iota((keys, rows), 0)
    count = jnp.zeros((keys, rows), F32)
    for k in range(crossings):
        count = count + jnp.where(ids == key[k : k + 1, :], 1.0, 0.0)
    widen = (iota((rows, rows * SUB), 1) // SUB == iota((rows, rows * SUB), 0)).astype(BF16)
    spread = dot(count.astype(BF16), widen)
    step = WIDE // SUB
    for c in range(keys // step):
        fwd[c * WIDE : (c + 1) * WIDE, :] = repeat_rows(spread[c * step : (c + 1) * step])

    pl.semaphore_wait(barrier, len(peers))

    def remote(src, dst, sem_s, sem_r, peer):
        return pltpu.make_async_remote_copy(
            src_ref=src, dst_ref=dst, send_sem=sem_s, recv_sem=sem_r,
            device_id=peer, device_id_type=MESH,
        )

    def halo(i, src, dst, peer):
        return remote(src, dst, halo_send.at[i], halo_recv.at[i], peer)

    halos = [
        halo(0, vol_ref.at[pl.ds(0, 1)], vv.at[pl.ds(rows + 1, 1)], (layer, t_prev)),
        halo(1, vol_ref.at[pl.ds(rows - 1, 1)], vv.at[pl.ds(0, 1)], (layer, t_next)),
    ]
    for copy in halos:
        copy.start()

    for c in range(parts):
        loads[c].wait()
        for z in range(zt):
            part = vv[1 + c * piece : 1 + (c + 1) * piece, z * SUB : (z + 1) * SUB, :]
            vb[c * piece * SUB : (c + 1) * piece * SUB, z * px : (z + 1) * px] = part.reshape(
                piece * SUB, px
            ).astype(BF16)
    edge_lo[...] = vv[1 : rows + 1, 0, :]
    edge_hi[...] = vv[1 : rows + 1, slices - 1, :]
    more = [
        halo(2, edge_lo, next_z.at[pl.ds(0, rows)], (z_prev, pos)),
        halo(3, edge_hi, prev_z.at[pl.ds(0, rows)], (z_next, pos)),
        halo(4, edge_hi.at[pl.ds(0, SUB)], prev_z.at[pl.ds(rows, SUB)], (z_next, t_prev)),
        halo(5, edge_lo.at[pl.ds(rows - SUB, SUB)], next_z.at[pl.ds(rows, SUB)], (z_prev, t_next)),
    ]
    for copy in more:
        copy.start()
    halos += more

    load_table.wait()

    per = WIDE // ts
    total = jnp.zeros((zt * ts, rays), F32)
    for c in range(nfoot // per):
        summed = dot(fwd[c * WIDE : (c + 1) * WIDE, :], vb[...])
        turned = jnp.concatenate(
            [
                jnp.concatenate(
                    [summed[f * ts : (f + 1) * ts, z * px : (z + 1) * px] for z in range(zt)], axis=0
                )
                for f in range(per)
            ],
            axis=1,
        ).astype(BF16)
        total = total + dot(turned, table_ref[c * per * px : (c + 1) * per * px, :])
    total = total.reshape(zt, touch, SUB, rays)
    partial = [total[:, t].reshape(slices, rays) for t in range(touch)]
    for o in range(owners):
        send[o] = sum(place[o][t] * partial[t] for t in range(touch)).astype(WIRE)

    there = []
    for d in range(1, owners):
        peer = lax.rem(pos + d, owners)
        there.append(
            remote(send.at[peer], recv.at[pos], part_send.at[d], part_recv.at[d], (layer, peer))
        )
    for copy in there:
        copy.start()
    recv[pl.ds(pos, 1)] = send[pl.ds(pos, 1)]

    last_row = pos == owners - 1
    last_slice = layer == slabs - 1
    sub = iota((slices, px), 0)
    lane = iota((slices, px), 1)
    after = iota((rows, px), 0)

    def inverse(a, b, c):
        return lax.rsqrt(a * a + b * b + c * c + smoothing)

    def column(v, where):
        return jnp.where(where == px - 1, 0.0, pltpu.roll(v, px - 1, 1) - v)

    def slice_flux(corner):
        lower = prev_z[0:rows, :]
        g_z = edge_lo[...] - lower
        below = pltpu.roll(lower, rows - 1, 0)
        if corner is not None:
            below = jnp.where(after == rows - 1, jnp.where(last_row, lower, corner), below)
        flux = g_z * inverse(below - lower, g_z, column(lower, iota((rows, px), 1)))
        prev_flux[...] = jnp.where(layer == 0, 0.0, flux)

    def next_slice(v, edge):
        return jnp.where(sub == slices - 1, edge, pltpu.roll(v, slices - 1, 0)) - v

    def tv_row(r, flux, v, below):
        g_r = below - v
        g_z = next_slice(v, upper[pl.ds(r, 1), :])
        g_c = column(v, lane)
        inv = inverse(g_r, g_z, g_c)
        f_r, f_z, f_c = g_r * inv, g_z * inv, g_c * inv
        came = jnp.where(sub == 0, prev_flux[pl.ds(r, 1), :], pltpu.roll(f_z, 1, 0))
        variation = (flux - f_r) + (came - f_z) + (pltpu.roll(f_c, 1, 1) - f_c)
        base[r] = v - (step_length * variation_weight) * variation
        return f_r

    def tv_rows(first, flux, final=False):
        for j in range(TOGETHER):
            v, below = vv[first + j + 1], vv[first + j + 2]
            if final and j == TOGETHER - 1:
                below = jnp.where(last_row, v, below)
            flux = tv_row(first + j, flux, v, below)
        return flux

    def tv_step(i, flux):
        return tv_rows(i * TOGETHER, flux)

    for copy in halos[2:4]:
        copy.wait_recv()
    upper[...] = jnp.where(last_slice, edge_hi[...], next_z[0:rows, :])
    slice_flux(None)
    flux = lax.fori_loop(0, early, tv_step, jnp.zeros((slices, px), F32))

    for copy in there:
        copy.wait_recv()
    residual = []
    for l in range(owned):
        own = sum(
            jnp.where(locals_[n] == l, 1.0, 0.0) * recv[n].astype(F32) for n in range(owners)
        )
        residual.append((wt_ref[l] * (own - meas_ref[l])).astype(BF16).astype(F32))
    for n in range(owners):
        picked = sum(jnp.where(locals_[n] == l, 1.0, 0.0) * residual[l] for l in range(owned))
        back_send[n] = picked.astype(BF16)
    home = []
    for d in range(1, owners):
        peer = lax.rem(pos + d, owners)
        home.append(
            remote(
                back_send.at[peer], back_recv.at[pos], res_send.at[d], res_recv.at[d], (layer, peer)
            )
        )
    for copy in home:
        copy.start()
    back_recv[pl.ds(pos, 1)] = back_send[pl.ds(pos, 1)]

    for copy in halos[:2] + halos[4:]:
        copy.wait_recv()
    slice_flux(prev_z[rows : rows + 1, :])
    before = vv[0]
    corner = jnp.where(last_slice, before[slices - 1 : slices, :], next_z[rows + SUB - 1 : rows + SUB, :])
    g_r = vv[1] - before
    came = g_r * inverse(g_r, next_slice(before, corner), column(before, lane))
    base[0] = base[0] - (step_length * variation_weight) * jnp.where(pos == 0, 0.0, came)
    steps = rows // TOGETHER
    flux = lax.fori_loop(early, steps - 1, tv_step, flux)
    tv_rows((steps - 1) * TOGETHER, flux, True)
    write_base = pltpu.make_async_copy(base, base_out, out_sem.at[0])
    write_base.start()

    widen = (iota((keys, keys * SUB), 1) // SUB == iota((keys, keys * SUB), 0)).astype(BF16)
    spread = dot(count.T.astype(BF16), widen)
    step = math.gcd(rows, 16)
    for c in range(rows // step):
        bwd[c * step * SUB : (c + 1) * step * SUB, :] = repeat_rows(
            spread[c * step : (c + 1) * step]
        )
    write_back = pltpu.make_async_copy(bwd, back_out, out_sem.at[1])
    write_back.start()

    for copy in home:
        copy.wait_recv()
    arrived = []
    for t in range(touch):
        one = sum(place[o][t] * back_recv[o].astype(F32) for o in range(owners))
        arrived.append(one.reshape(zt, SUB, rays))
    resid_ref[...] = jnp.stack(arrived, axis=1).reshape(zt * ts, rays).astype(BF16)
    write_base.wait()
    write_back.wait()
    for copy in halos + there + home:
        copy.wait_send()


def update_kernel(touch, resid_ref, table_ref, back_ref, base_ref, out_ref, grads):
    rows, slices, px = base_ref.shape
    nfoot = table_ref.shape[0] // px
    zt = slices // SUB
    ts = touch * SUB

    @pl.when(pl.program_id(0) == 0)
    def _():
        per = WIDE // px
        for c in range(nfoot // per):
            piece = lax.dot_general(
                resid_ref[...],
                table_ref[c * WIDE : (c + 1) * WIDE, :],
                (((1,), (1,)), ((), ())),
                preferred_element_type=F32,
            )
            for f in range(per):
                for z in range(zt):
                    at = (c * per + f) * ts
                    grads[at : at + ts, z * px : (z + 1) * px] = piece[
                        z * ts : (z + 1) * ts, f * px : (f + 1) * px
                    ].astype(BF16)

    grad = dot(back_ref[...], grads[...])
    for z in range(zt):
        at = slice(z * SUB, (z + 1) * SUB)
        one = grad[:, z * px : (z + 1) * px].reshape(rows, SUB, px)
        out_ref[:, at, :] = jnp.maximum(base_ref[:, at, :] - step_length * one, 0.0)


def per_device(owners, slabs, volume, footprints, foot_index, ray_block, ray_slot, measured, weights):
    rows, slices, px = volume.shape
    nfoot, _, rays = footprints.shape
    touch = owners // 2
    keys = nfoot * touch
    zt = slices // SUB
    table = footprints.reshape(nfoot * px, rays)
    any_space = pl.BlockSpec(memory_space=pl.ANY)
    vmem = pl.BlockSpec(memory_space=pltpu.VMEM)
    smem = pl.BlockSpec(memory_space=pltpu.SMEM)
    dma = pltpu.SemaphoreType.DMA
    base, back, resid = pl.pallas_call(
        functools.partial(exchange_kernel, touch, owners, slabs, rows // TOGETHER // 2),
        out_shape=(
            jax.ShapeDtypeStruct(volume.shape, F32),
            jax.ShapeDtypeStruct((rows * SUB, keys * SUB), BF16),
            jax.ShapeDtypeStruct((zt * touch * SUB, rays), BF16),
        ),
        in_specs=[any_space, any_space, vmem, vmem, smem, vmem, vmem],
        out_specs=(any_space, any_space, vmem),
        scratch_shapes=[
            pltpu.VMEM(table.shape, BF16),
            pltpu.VMEM((rows + 2, slices, px), F32),
            pltpu.VMEM((rows * SUB, zt * px), BF16),
            pltpu.VMEM((keys * SUB, rows * SUB), BF16),
            pltpu.VMEM((rows * SUB, keys * SUB), BF16),
            pltpu.VMEM((rows, slices, px), F32),
            pltpu.VMEM((rows, px), F32),
            pltpu.VMEM((rows, px), F32),
            pltpu.VMEM((rows + SUB, px), F32),
            pltpu.VMEM((rows + SUB, px), F32),
            pltpu.VMEM((rows, px), F32),
            pltpu.VMEM((rows, px), F32),
            pltpu.VMEM((owners, slices, rays), WIRE),
            pltpu.VMEM((owners, slices, rays), WIRE),
            pltpu.VMEM((owners, slices, rays), BF16),
            pltpu.VMEM((owners, slices, rays), BF16),
            dma((5,)),
            dma((2,)),
            dma((6,)),
            dma((6,)),
            dma((owners,)),
            dma((owners,)),
            dma((owners,)),
            dma((owners,)),
        ],
        compiler_params=pltpu.CompilerParams(
            collective_id=0, has_side_effects=True, vmem_limit_bytes=VMEM_LIMIT
        ),
    )(volume, table, foot_index.T, ray_block.T, ray_slot, measured, weights)
    some = math.gcd(rows, WIDE // SUB)
    steps = rows // some
    return pl.pallas_call(
        functools.partial(update_kernel, touch),
        grid=(steps,),
        out_shape=jax.ShapeDtypeStruct(volume.shape, F32),
        in_specs=[
            pl.BlockSpec(resid.shape, lambda i: (0, 0)),
            pl.BlockSpec(table.shape, lambda i: (0, 0)),
            pl.BlockSpec((some * SUB, keys * SUB), lambda i: (i, 0)),
            pl.BlockSpec((some, slices, px), lambda i: (i, 0, 0)),
        ],
        out_specs=pl.BlockSpec((some, slices, px), lambda i: (i, 0, 0)),
        scratch_shapes=[pltpu.VMEM((keys * SUB, zt * px), BF16)],
        compiler_params=pltpu.CompilerParams(vmem_limit_bytes=VMEM_LIMIT),
    )(resid, table, back, base)


def solution(mesh):
    in_specs = (
        P("tile", "slab", None),
        P(),
        P("tile", None),
        P(),
        P(),
        P("tile", "slab", None),
        P("tile", "slab", None),
    )
    out_specs = P("tile", "slab", None)
    body = functools.partial(per_device, mesh.shape["tile"], mesh.shape["slab"])
    return jax.shard_map(body, mesh=mesh, in_specs=in_specs, out_specs=out_specs, check_vma=False)
```
